32 devices in a mesh: row: 8 (over z, core), col: 4 (over y, x).
Axes of the slice: x: 2, y: 2, z: 4, core: 2. Of those that a mesh axis runs over, the one named last changes fastest.
Arguments:
- diag_rows: bfloat16 [8, 16, 512, 512], P('row', 'col'), may hold values from -0.12988281 to 0.12988281
- next_rows: bfloat16 [8, 16, 128, 512], P('row', 'col'), may hold values from -6 to 6
- routes: int32 [8, 4, 4], P('row', 'col'), may hold values from 0 to 3, each once within a row
- diag_blocks: bfloat16 [8, 4, 512, 512], P('row', 'col'), as said below
- panel_blocks: bfloat16 [8, 4, 128, 512], P('row', 'col'), may hold values from -6 to 6
Outputs:
- diag_factor: bfloat16 [8, 4, 512, 512], P('row', 'col')
- panel_factor: bfloat16 [8, 4, 128, 512], P('row', 'col')
The draws below stay inside these ranges and needn't reach their ends.
Inputs may be any that keep to these rules, and one draw needn't show every extreme that they name: `routes`: the 4 sources of one device name every target column exactly once. `diag_blocks`: every block is symmetric positive definite with eigenvalues of at least 0.5 before rounding.
All inputs are finite; a program needn't handle non-finite values.
Results may differ from the reference program's by a relative error of at most 0.001.
Values may be sent and summed in bfloat16 or wider, within the bound.
A program may use at most 128 MiB of HBM per device.

```python
import jax
import jax.numpy as jnp
from jax import lax

BS = 512
RB = 128
PROWS = 8
PCOLS = 4
KD = 4


def draw_diag_blocks(key, part):
    key_rows, key_shift = jax.random.split(key, 2)
    raw_rows = jax.random.normal(key_rows, (PROWS, PCOLS, BS, BS), jnp.float32)
    gram_part = jnp.einsum('gcik,gcjk->gcij', raw_rows, raw_rows) / BS
    diag_shift = jax.random.uniform(key_shift, (PROWS, PCOLS, BS), jnp.float32, 0.5, 2.0)
    return (gram_part + diag_shift[..., None] * jnp.eye(BS, dtype=jnp.float32)).astype(jnp.bfloat16)


def levels(own_key, dims, cuts, smallest, largest):
    gain = 1.0
    for position, shards_of in cuts:
        draws = jax.random.uniform(jax.random.fold_in(jax.random.fold_in(own_key, 6), position), (shards_of,), jnp.float32, smallest / len(cuts), largest / len(cuts))
        gain = gain * jnp.repeat(jnp.exp(draws), dims[position] // shards_of).reshape((-1,) + (1,) * (len(dims) - 1 - position))
    return gain


def noise(key, shape, scale, reach, cuts=(), kind=jnp.bfloat16):
    values = scale * jax.random.normal(key, shape, jnp.float32)
    if cuts:
        values = values * levels(key, shape, cuts, -0.22, 0.18)
    return jnp.clip(values, -reach, reach).astype(kind)


def setup_inputs(seed: int = 0) -> dict:
    arg_keys = jax.random.split(jax.random.key(seed), 6)
    return {
        "diag_rows": noise(arg_keys[0], (PROWS, PCOLS * KD, BS, BS), 0.022, 0.12988281, ((0, 8), (1, 4))),
        "next_rows": noise(arg_keys[1], (PROWS, PCOLS * KD, RB, BS), 1.0, 6.0, ((0, 8), (1, 4))),
        "routes": jax.vmap(lambda own: jax.random.permutation(own, PCOLS))(jax.random.split(arg_keys[2], PROWS * PCOLS)).reshape((PROWS, PCOLS, KD)).astype(jnp.int32),
        "diag_blocks": draw_diag_blocks(jax.random.fold_in(arg_keys[5], 71), 0),
        "panel_blocks": noise(arg_keys[4], (PROWS, PCOLS, RB, BS), 1.0, 6.0, ((0, 8), (1, 4))),
    }


def reference(diag_rows, next_rows, routes, diag_blocks, panel_blocks):
    columns = diag_blocks.shape[1]
    width = diag_blocks.shape[2]
    panel_height = panel_blocks.shape[2]
    lower_rows = jnp.roll(next_rows, -1, axis=0)
    lower_panels = jnp.roll(panel_blocks, -1, axis=0)

    def row_work(index):
        upper = diag_rows[index]
        lower = lower_rows[index]
        target = routes[index].reshape(-1).astype(jnp.int32)

        def step(carry, item):
            gram_acc, cross_acc = carry
            block_x, block_y, where = item
            gram_acc = gram_acc.at[where].add(jnp.dot(block_x.astype(jnp.float32), block_x.T.astype(jnp.float32), preferred_element_type=jnp.float32))
            cross_acc = cross_acc.at[where].add(jnp.dot(block_y.astype(jnp.float32), block_x.T.astype(jnp.float32), preferred_element_type=jnp.float32))
            return ((gram_acc, cross_acc), None)
        empty_gram = jnp.zeros((columns, width, width), jnp.float32)
        empty_cross = jnp.zeros((columns, panel_height, width), jnp.float32)
        (gram_sum, cross_sum), unused = lax.scan(step, (empty_gram, empty_cross), (upper, lower, target))
        factor = jax.vmap(jnp.linalg.cholesky)(diag_blocks[index].astype(jnp.float32) + gram_sum)
        total = lower_panels[index].astype(jnp.float32) + cross_sum

        def solve_one(tri, rhs):
            return jax.scipy.linalg.solve_triangular(tri, rhs.T, lower=True).T
        solved = jax.vmap(solve_one)(factor, total)
        return (factor.astype(jnp.bfloat16), solved.astype(jnp.bfloat16))
    factors, panels = lax.map(row_work, jnp.arange(diag_blocks.shape[0], dtype=jnp.int32))
    return (factors, jnp.roll(panels, 1, axis=0))
```

```python
import functools

import jax
import jax.numpy as jnp
from jax import lax
from jax.experimental import pallas as pl
from jax.experimental.pallas import tpu as pltpu
from jax.sharding import PartitionSpec as P

TILE = 128
SMALL = 16
NT = (((1,), (1,)), ((), ()))
TN = (((0,), (0,)), ((), ()))


def split(value):
    high = value.astype(jnp.bfloat16)
    low = (value - high.astype(jnp.float32)).astype(jnp.bfloat16)
    return high, low


def dot(left, right, dims):
    return lax.dot_general(left, right, dims, preferred_element_type=jnp.float32)


def product(left, right, axis, dims):
    left_high, left_low = split(left)
    right_high, right_low = split(right)
    return dot(
        jnp.concatenate([left_high, left_high, left_low], axis=axis),
        jnp.concatenate([right_high, right_low, right_high], axis=axis),
        dims,
    )


def eliminate(work, spread):
    full = (8, 2 * TILE)
    lane = lax.broadcasted_iota(jnp.int32, (SMALL, TILE), 1)

    def step(block, carry):
        start = pl.multiple_of(block * SMALL, SMALL)
        own = work.at[pl.ds(start, SMALL), :]
        pivots = pltpu.roll(own[:, :TILE], lax.rem(TILE - start, TILE), 1)
        for m in range(SMALL):
            spread[m * SMALL : (m + 1) * SMALL, :] = jnp.broadcast_to(
                pivots[:, m : m + 1], (SMALL, TILE)
            )
        value = {}
        for m in range(SMALL):
            for i in range(m, SMALL):
                at = m * SMALL + i
                value[i, m] = jnp.broadcast_to(spread[at : at + 1, :], (8, TILE))
        rows = [jnp.broadcast_to(own[i : i + 1, :], full) for i in range(SMALL)]
        for m in range(SMALL):
            scale = lax.rsqrt(value[m, m])
            rows[m] = rows[m] * jnp.concatenate([scale, scale], axis=1)
            own[m : m + 1, :] = rows[m][0:1, :]
            column = {i: value[i, m] * scale for i in range(m + 1, SMALL)}
            for k in range(m + 1, SMALL):
                for i in range(k, SMALL):
                    value[i, k] = value[i, k] - column[i] * column[k]
                rows[k] = rows[k] - jnp.concatenate([column[k], column[k]], axis=1) * rows[m]
        solved = own[...]
        high, low = split(solved)
        left_high, left_low = split(jnp.where(lane >= start + SMALL, solved[:, :TILE], 0.0))
        update = dot(
            jnp.concatenate([left_high, left_high, left_low], axis=0),
            jnp.concatenate([high, low, high], axis=0),
            TN,
        )
        work[...] = work[...] - update
        return carry

    lax.fori_loop(0, TILE // SMALL, step, 0)


def factor_kernel(x_ref, y_ref, diag_ref, panel_ref, factor_ref, solved_ref, total, work, spread):
    sources, width, depth = x_ref.shape
    height = y_ref.shape[1]
    tiles = width // TILE
    for q in range(tiles):
        cols = slice(q * TILE, (q + 1) * TILE)
        gram = diag_ref[q * TILE :, cols].astype(jnp.float32)
        cross = panel_ref[:, cols].astype(jnp.float32)
        for s in range(sources):
            right = x_ref[s, cols, :]
            gram = gram + dot(x_ref[s, q * TILE :, :], right, NT)
            cross = cross + dot(y_ref[s], right, NT)
        total[q * TILE : width, cols] = gram
        total[width:, cols] = cross
    row = lax.broadcasted_iota(jnp.int32, (TILE, TILE), 0)
    lane = lax.broadcasted_iota(jnp.int32, (TILE, TILE), 1)
    for q in range(tiles):
        low, high = q * TILE, (q + 1) * TILE
        work[:, :TILE] = total[low:high, low:high]
        work[:, TILE:] = (row == lane).astype(jnp.float32)
        eliminate(work, spread)
        upper = jnp.where(row <= lane, work[:, :TILE], 0.0)
        factor_ref[low:high, low:high] = upper.T.astype(jnp.bfloat16)
        if q + 1 < tiles:
            factor_ref[low:high, high:] = jnp.zeros((TILE, width - high), jnp.bfloat16)
        below = product(total[high:, low:high], work[:, TILE:], 1, NT)
        if q + 1 < tiles:
            factor_ref[high:, low:high] = below[: width - high].astype(jnp.bfloat16)
        solved_ref[:, low:high] = below[width - high :].astype(jnp.bfloat16)
        if q + 1 < tiles:
            total[high:, high:] = total[high:, high:] - product(below, below[: width - high], 1, NT)


def factor_and_solve(x, y, diag, panel):
    sources, width, depth = x.shape
    height = y.shape[1]
    vmem = pl.BlockSpec(memory_space=pltpu.VMEM)
    return pl.pallas_call(
        factor_kernel,
        out_shape=(
            jax.ShapeDtypeStruct((width, width), jnp.bfloat16),
            jax.ShapeDtypeStruct((height, width), jnp.bfloat16),
        ),
        in_specs=[vmem] * 4,
        out_specs=(vmem, vmem),
        scratch_shapes=[
            pltpu.VMEM((width + height, width), jnp.float32),
            pltpu.VMEM((TILE, 2 * TILE), jnp.float32),
            pltpu.VMEM((SMALL * SMALL, TILE), jnp.float32),
        ],
        compiler_params=pltpu.CompilerParams(vmem_limit_bytes=48 * 1024 * 1024),
    )(x, y, diag, panel)


def from_behind(value, axis, steps):
    count = lax.axis_size(axis)
    pairs = [(source, (source + steps) % count) for source in range(count)]
    return lax.ppermute(value, axis, pairs)


def place_slots(sources, targets, columns):
    selector = (targets[0, 0, :][:, None] == jnp.arange(columns, dtype=jnp.int32)[None, :]).astype(
        jnp.bfloat16
    )
    placed = jnp.einsum("sj,sab->jab", selector, sources, preferred_element_type=jnp.float32)
    return placed.astype(jnp.bfloat16)


def body(diag_rows, next_rows, routes, diag_blocks, panel_blocks):
    columns = lax.axis_size("col")
    send_diag = place_slots(diag_rows[0], routes, columns)
    lifted_next, panel_source = from_behind((next_rows, panel_blocks), "row", -1)
    send_next = place_slots(lifted_next[0], routes, columns)
    recv_diag, recv_next = (
        lax.all_to_all(send_diag, "col", split_axis=0, concat_axis=0, tiled=True),
        lax.all_to_all(send_next, "col", split_axis=0, concat_axis=0, tiled=True),
    )
    factor, solved = factor_and_solve(recv_diag, recv_next, diag_blocks[0, 0], panel_source[0, 0])
    panel_out = from_behind(solved, "row", 1)
    return (factor[None, None], panel_out[None, None])


def solution(mesh):
    placed = (
        P("row", "col", None, None),
        P("row", "col", None, None),
        P("row", "col", None),
        P("row", "col", None, None),
        P("row", "col", None, None),
    )
    return jax.shard_map(
        body,
        mesh=mesh,
        in_specs=placed,
        out_specs=(P("row", "col", None, None), P("row", "col", None, None)),
        check_vma=False,
    )
```

```python
import jax
import jax.numpy as jnp
from jax import lax
from jax.experimental import pallas as pl
from jax.experimental.pallas import tpu as pltpu
from jax.sharding import PartitionSpec as P

TILE = 128
SMALL = 16
MESH = pl.DeviceIdType.MESH
NT = (((1,), (1,)), ((), ()))
TN = (((0,), (0,)), ((), ()))


def split(value):
    high = value.astype(jnp.bfloat16)
    low = (value - high.astype(jnp.float32)).astype(jnp.bfloat16)
    return high, low


def dot(left, right, dims):
    return lax.dot_general(left, right, dims, preferred_element_type=jnp.float32)


def product(left, right, axis, dims):
    left_high, left_low = split(left)
    right_high, right_low = split(right)
    return dot(
        jnp.concatenate([left_high, left_high, left_low], axis=axis),
        jnp.concatenate([right_high, right_low, right_high], axis=axis),
        dims,
    )


def eliminate(work, spread):
    full = (8, 2 * TILE)
    lane = lax.broadcasted_iota(jnp.int32, (SMALL, TILE), 1)

    def step(block, carry):
        start = pl.multiple_of(block * SMALL, SMALL)
        own = work.at[pl.ds(start, SMALL), :]
        pivots = pltpu.roll(own[:, :TILE], lax.rem(TILE - start, TILE), 1)
        for m in range(SMALL):
            spread[m * SMALL : (m + 1) * SMALL, :] = jnp.broadcast_to(
                pivots[:, m : m + 1], (SMALL, TILE)
            )
        value = {}
        for m in range(SMALL):
            for i in range(m, SMALL):
                at = m * SMALL + i
                value[i, m] = jnp.broadcast_to(spread[at : at + 1, :], (8, TILE))
        rows = [jnp.broadcast_to(own[i : i + 1, :], full) for i in range(SMALL)]
        for m in range(SMALL):
            scale = lax.rsqrt(value[m, m])
            rows[m] = rows[m] * jnp.concatenate([scale, scale], axis=1)
            own[m : m + 1, :] = rows[m][0:1, :]
            column = {i: value[i, m] * scale for i in range(m + 1, SMALL)}
            for k in range(m + 1, SMALL):
                for i in range(k, SMALL):
                    value[i, k] = value[i, k] - column[i] * column[k]
                rows[k] = rows[k] - jnp.concatenate([column[k], column[k]], axis=1) * rows[m]
        solved = own[...]
        high, low = split(solved)
        left_high, left_low = split(jnp.where(lane >= start + SMALL, solved[:, :TILE], 0.0))
        update = dot(
            jnp.concatenate([left_high, left_high, left_low], axis=0),
            jnp.concatenate([high, low, high], axis=0),
            TN,
        )
        work[...] = work[...] - update
        return carry

    lax.fori_loop(0, TILE // SMALL, step, 0)


def level_kernel(
    x_ref, y_ref, routes_ref, diag_ref, panel_ref, factor_ref, home_ref,
    x_send, x_recv, y_lift, y_send, y_recv, panel_recv, solved_send, solved_recv,
    total, inverse, work, spread,
    x_out, x_in, y_out, y_in, row_out, row_in, home_out, home_in,
):
    sources, width, depth = x_ref.shape
    tiles = width // TILE
    columns, rows = lax.axis_size("col"), lax.axis_size("row")
    my_column, my_row = lax.axis_index("col"), lax.axis_index("row")
    ahead, behind = lax.rem(my_row + 1, rows), lax.rem(my_row + rows - 1, rows)
    partner = [lax.rem(my_column + d, columns) for d in range(columns)]

    barrier = pltpu.get_barrier_semaphore()
    for d in range(1, columns):
        pl.semaphore_signal(barrier, inc=1, device_id={"col": partner[d]}, device_id_type=MESH)
    for other in (ahead, behind):
        pl.semaphore_signal(barrier, inc=1, device_id={"row": other}, device_id_type=MESH)

    slot = []
    for d in range(columns):
        found = jnp.int32(0)
        for s in range(sources):
            found = jnp.where(routes_ref[s] == partner[d], jnp.int32(s), found)
        slot.append(found)

    def chunk(q):
        return slice(q * TILE, (q + 1) * TILE)

    def stage(q):
        for d in range(1, columns):
            x_send[d - 1, chunk(q), :] = x_ref[slot[d], chunk(q), :]
        x_recv[0, chunk(q), :] = x_ref[slot[0], chunk(q), :]

    def remote(source, target, out, into, device):
        return pltpu.make_async_remote_copy(
            src_ref=source, dst_ref=target, send_sem=out, recv_sem=into,
            device_id=device, device_id_type=MESH,
        )

    x_copies = [
        [
            remote(
                x_send.at[d - 1, chunk(q), :], x_recv.at[d, chunk(q), :],
                x_out.at[q, d - 1], x_in.at[q, d - 1], {"col": partner[d]},
            )
            for d in range(1, columns)
        ]
        for q in range(tiles)
    ]
    lift = remote(y_ref, y_lift, row_out.at[0], row_in.at[0], {"row": behind})
    panel_copy = remote(panel_ref, panel_recv, row_out.at[1], row_in.at[1], {"row": behind})
    y_copies = [
        remote(y_send.at[d - 1], y_recv.at[d], y_out.at[d - 1], y_in.at[d - 1], {"col": partner[d]})
        for d in range(1, columns)
    ]
    home_copies = [
        remote(
            solved_send.at[q], solved_recv.at[q], home_out.at[q], home_in.at[q], {"row": ahead}
        )
        for q in range(tiles)
    ]

    stage(0)
    pl.semaphore_wait(barrier, columns + 1)
    for copy in x_copies[0]:
        copy.start()
    lift.start()
    panel_copy.start()
    for q in range(1, tiles):
        stage(q)
        for copy in x_copies[q]:
            copy.start()

    row = lax.broadcasted_iota(jnp.int32, (TILE, TILE), 0)
    lane = lax.broadcasted_iota(jnp.int32, (TILE, TILE), 1)
    for q in range(tiles):
        low, high = q * TILE, (q + 1) * TILE
        for copy in x_copies[q]:
            copy.wait_recv()
        gram = diag_ref[low:high, :high].astype(jnp.float32)
        for s in range(columns):
            gram = gram + dot(x_recv[s, low:high, :], x_recv[s, :high, :], NT)
        total[low:high, :high] = gram
        for p in range(q):
            left = product(total[low:high, chunk(p)], inverse[p], 1, NT)
            total[low:high, chunk(p)] = left
            factor_ref[low:high, chunk(p)] = left.astype(jnp.bfloat16)
            total[low:high, (p + 1) * TILE : high] = total[
                low:high, (p + 1) * TILE : high
            ] - product(left, total[(p + 1) * TILE : high, chunk(p)], 1, NT)
        work[:, :TILE] = total[low:high, low:high]
        work[:, TILE:] = (row == lane).astype(jnp.float32)
        eliminate(work, spread)
        upper = jnp.where(row <= lane, work[:, :TILE], 0.0)
        factor_ref[low:high, low:high] = upper.T.astype(jnp.bfloat16)
        if q + 1 < tiles:
            factor_ref[low:high, high:] = jnp.zeros((TILE, width - high), jnp.bfloat16)
        inverse[q] = work[:, TILE:]
        if q == 0:
            lift.wait_recv()
            for d in range(1, columns):
                y_send[d - 1] = y_lift[slot[d]]
                y_copies[d - 1].start()
            y_recv[0] = y_lift[slot[0]]

    panel_copy.wait_recv()
    for copy in y_copies:
        copy.wait_recv()
    cross = panel_recv[...].astype(jnp.float32)
    for s in range(columns):
        cross = cross + dot(y_recv[s], x_recv[s], NT)
    for q in range(tiles):
        solved = product(cross[:, :TILE], inverse[q], 1, NT)
        solved_send[q] = solved.astype(jnp.bfloat16)
        home_copies[q].start()
        if q + 1 < tiles:
            cross = cross[:, TILE:] - product(solved, total[(q + 1) * TILE :, chunk(q)], 1, NT)
    for q in range(tiles):
        home_copies[q].wait_recv()
        home_ref[:, chunk(q)] = solved_recv[q]

    for copy in [*sum(x_copies, []), lift, panel_copy, *y_copies, *home_copies]:
        copy.wait_send()


def body(diag_rows, next_rows, routes, diag_blocks, panel_blocks):
    x, y, diag, panel = diag_rows[0], next_rows[0], diag_blocks[0, 0], panel_blocks[0, 0]
    sources, width, depth = x.shape
    height = y.shape[1]
    columns = lax.axis_size("col")
    tiles = width // TILE
    kind = x.dtype
    vmem = pl.BlockSpec(memory_space=pltpu.VMEM)
    dma = pltpu.SemaphoreType.DMA
    factor, home = pl.pallas_call(
        level_kernel,
        out_shape=(
            jax.ShapeDtypeStruct((width, width), kind),
            jax.ShapeDtypeStruct((height, width), kind),
        ),
        in_specs=[vmem, vmem, pl.BlockSpec(memory_space=pltpu.SMEM), vmem, vmem],
        out_specs=(vmem, vmem),
        scratch_shapes=[
            pltpu.VMEM((columns - 1, width, depth), kind),
            pltpu.VMEM((columns, width, depth), kind),
            pltpu.VMEM((sources, height, depth), kind),
            pltpu.VMEM((columns - 1, height, depth), kind),
            pltpu.VMEM((columns, height, depth), kind),
            pltpu.VMEM((height, width), kind),
            pltpu.VMEM((tiles, height, TILE), kind),
            pltpu.VMEM((tiles, height, TILE), kind),
            pltpu.VMEM((width, width), jnp.float32),
            pltpu.VMEM((tiles, TILE, TILE), jnp.float32),
            pltpu.VMEM((TILE, 2 * TILE), jnp.float32),
            pltpu.VMEM((SMALL * SMALL, TILE), jnp.float32),
            dma((tiles, columns - 1)),
            dma((tiles, columns - 1)),
            dma((columns - 1,)),
            dma((columns - 1,)),
            dma((2,)),
            dma((2,)),
            dma((tiles,)),
            dma((tiles,)),
        ],
        compiler_params=pltpu.CompilerParams(
            collective_id=0, has_side_effects=True, vmem_limit_bytes=56 * 1024 * 1024
        ),
    )(x, y, routes[0, 0], diag, panel)
    return (factor[None, None], home[None, None])


def solution(mesh):
    placed = (
        P("row", "col", None, None),
        P("row", "col", None, None),
        P("row", "col", None),
        P("row", "col", None, None),
        P("row", "col", None, None),
    )
    return jax.shard_map(
        body,
        mesh=mesh,
        in_specs=placed,
        out_specs=(P("row", "col", None, None), P("row", "col", None, None)),
        check_vma=False,
    )
```

```python
import jax
import jax.numpy as jnp
from jax import lax
from jax.experimental import pallas as pl
from jax.experimental.pallas import tpu as pltpu
from jax.sharding import PartitionSpec as P

TILE = 128
SMALL = 16
HALF = SMALL // 2
MESH = pl.DeviceIdType.MESH
NT = (((1,), (1,)), ((), ()))
TN = (((0,), (0,)), ((), ()))


def split(value):
    high = value.astype(jnp.bfloat16)
    low = (value - high.astype(jnp.float32)).astype(jnp.bfloat16)
    return high, low


def dot(left, right, dims):
    return lax.dot_general(left, right, dims, preferred_element_type=jnp.float32)


def product(left, right, axis, dims):
    left_high, left_low = split(left)
    right_high, right_low = split(right)
    return dot(
        jnp.concatenate([left_high, left_high, left_low], axis=axis),
        jnp.concatenate([right_high, right_low, right_high], axis=axis),
        dims,
    )


def eliminate(work, spread):
    full = (HALF, 2 * TILE)
    lane = lax.broadcasted_iota(jnp.int32, (SMALL, TILE), 1)

    def step(block, carry):
        start = pl.multiple_of(block * SMALL, SMALL)
        own = work.at[pl.ds(start, SMALL), :]
        pivots = pltpu.roll(own[:, :TILE], lax.rem(TILE - start, TILE), 1)
        tail = {}
        lower = {}
        for m in range(SMALL):
            wide = jnp.broadcast_to(pivots[:, m : m + 1], (SMALL, TILE))
            if m < HALF:
                spread[m * SMALL : m * SMALL + HALF, :] = wide[:HALF]
                lower[m] = wide[HALF:]
            else:
                tail[m] = wide[HALF:]
        rows = [jnp.broadcast_to(own[i : i + 1, :], full) for i in range(SMALL)]

        def single(m, i):
            at = m * SMALL + i
            return jnp.broadcast_to(spread[at : at + 1, :], (HALF, TILE))

        def twice(part):
            return jnp.concatenate([part, part], axis=1)

        for base in (0, HALF):
            inside = range(base, base + HALF)
            value = {(i, m): single(m, i) for m in inside for i in range(m, base + HALF)}
            for m in inside:
                scale = lax.rsqrt(value[m, m])
                column = {i: value[i, m] * scale for i in range(m + 1, base + HALF)}
                for k in column:
                    for i in range(k, base + HALF):
                        value[i, k] = value[i, k] - column[i] * column[k]
                rows[m] = rows[m] * twice(scale)
                own[m : m + 1, :] = rows[m][0:1, :]
                for k in column:
                    rows[k] = rows[k] - twice(column[k]) * rows[m]
                if base == 0:
                    lower[m] = lower[m] * scale
                    spread[m * SMALL + HALF : (m + 1) * SMALL, :] = lower[m]
                    for k in column:
                        lower[k] = lower[k] - column[k] * lower[m]
            if base == 0:
                for k in range(HALF, SMALL):
                    for m in range(HALF):
                        across = single(m, k)
                        tail[k] = tail[k] - across * lower[m]
                        rows[k] = rows[k] - twice(across) * rows[m]
                    spread[k * SMALL + HALF : (k + 1) * SMALL, :] = tail[k]
        solved = own[...]
        high, low = split(solved)
        left_high, left_low = split(jnp.where(lane >= start + SMALL, solved[:, :TILE], 0.0))
        update = dot(
            jnp.concatenate([left_high, left_high, left_low], axis=0),
            jnp.concatenate([high, low, high], axis=0),
            TN,
        )
        work[...] = work[...] - update
        return carry

    lax.fori_loop(0, TILE // SMALL, step, 0)


def level_kernel(
    x_ref, y_ref, routes_ref, diag_ref, panel_ref, factor_ref, home_ref,
    x_send, x_recv, y_lift, y_send, y_recv, panel_recv, solved_send, solved_recv,
    total, inverse, work, spread,
    x_out, x_in, y_out, y_in, row_out, row_in, home_out, home_in,
):
    sources, width, depth = x_ref.shape
    tiles = width // TILE
    columns, rows = lax.axis_size("col"), lax.axis_size("row")
    my_column, my_row = lax.axis_index("col"), lax.axis_index("row")
    ahead, behind = lax.rem(my_row + 1, rows), lax.rem(my_row + rows - 1, rows)
    partner = [lax.rem(my_column + d, columns) for d in range(columns)]

    barrier = pltpu.get_barrier_semaphore()
    for d in range(1, columns):
        pl.semaphore_signal(barrier, inc=1, device_id={"col": partner[d]}, device_id_type=MESH)
    for other in (ahead, behind):
        pl.semaphore_signal(barrier, inc=1, device_id={"row": other}, device_id_type=MESH)

    slot = []
    for d in range(columns):
        found = jnp.int32(0)
        for s in range(sources):
            found = jnp.where(routes_ref[s] == partner[d], jnp.int32(s), found)
        slot.append(found)

    def chunk(q):
        return slice(q * TILE, (q + 1) * TILE)

    def stage(q):
        for d in range(1, columns):
            x_send[d - 1, chunk(q), :] = x_ref[slot[d], chunk(q), :]
        x_recv[0, chunk(q), :] = x_ref[slot[0], chunk(q), :]

    def remote(source, target, out, into, device):
        return pltpu.make_async_remote_copy(
            src_ref=source, dst_ref=target, send_sem=out, recv_sem=into,
            device_id=device, device_id_type=MESH,
        )

    x_copies = [
        [
            remote(
                x_send.at[d - 1, chunk(q), :], x_recv.at[d, chunk(q), :],
                x_out.at[q, d - 1], x_in.at[q, d - 1], {"col": partner[d]},
            )
            for d in range(1, columns)
        ]
        for q in range(tiles)
    ]
    lift = remote(y_ref, y_lift, row_out.at[0], row_in.at[0], {"row": behind})
    panel_copy = remote(panel_ref, panel_recv, row_out.at[1], row_in.at[1], {"row": behind})
    y_copies = [
        remote(y_send.at[d - 1], y_recv.at[d], y_out.at[d - 1], y_in.at[d - 1], {"col": partner[d]})
        for d in range(1, columns)
    ]
    home_copies = [
        remote(
            solved_send.at[q], solved_recv.at[q], home_out.at[q], home_in.at[q], {"row": ahead}
        )
        for q in range(tiles)
    ]

    stage(0)
    pl.semaphore_wait(barrier, columns + 1)
    for copy in x_copies[0]:
        copy.start()
    lift.start()
    panel_copy.start()
    for q in range(1, tiles):
        stage(q)
        for copy in x_copies[q]:
            copy.start()

    row = lax.broadcasted_iota(jnp.int32, (TILE, TILE), 0)
    lane = lax.broadcasted_iota(jnp.int32, (TILE, TILE), 1)
    for q in range(tiles):
        low, high = q * TILE, (q + 1) * TILE
        for copy in x_copies[q]:
            copy.wait_recv()
        gram = diag_ref[low:high, :high].astype(jnp.float32)
        for s in range(columns):
            gram = gram + dot(x_recv[s, low:high, :], x_recv[s, :high, :], NT)
        total[low:high, :high] = gram
        for p in range(q):
            left = product(total[low:high, chunk(p)], inverse[p], 1, NT)
            total[low:high, chunk(p)] = left
            factor_ref[low:high, chunk(p)] = left.astype(jnp.bfloat16)
            total[low:high, (p + 1) * TILE : high] = total[
                low:high, (p + 1) * TILE : high
            ] - product(left, total[(p + 1) * TILE : high, chunk(p)], 1, NT)
        work[:, :TILE] = total[low:high, low:high]
        work[:, TILE:] = (row == lane).astype(jnp.float32)
        eliminate(work, spread)
        upper = jnp.where(row <= lane, work[:, :TILE], 0.0)
        factor_ref[low:high, low:high] = upper.T.astype(jnp.bfloat16)
        if q + 1 < tiles:
            factor_ref[low:high, high:] = jnp.zeros((TILE, width - high), jnp.bfloat16)
        inverse[q] = work[:, TILE:]
        if q == 0:
            lift.wait_recv()
            for d in range(1, columns):
                y_send[d - 1] = y_lift[slot[d]]
                y_copies[d - 1].start()
            y_recv[0] = y_lift[slot[0]]

    panel_copy.wait_recv()
    for copy in y_copies:
        copy.wait_recv()
    cross = panel_recv[...].astype(jnp.float32)
    for s in range(columns):
        cross = cross + dot(y_recv[s], x_recv[s], NT)
    for q in range(tiles):
        solved = product(cross[:, :TILE], inverse[q], 1, NT)
        solved_send[q] = solved.astype(jnp.bfloat16)
        home_copies[q].start()
        if q + 1 < tiles:
            cross = cross[:, TILE:] - product(solved, total[(q + 1) * TILE :, chunk(q)], 1, NT)
    for q in range(tiles):
        home_copies[q].wait_recv()
        home_ref[:, chunk(q)] = solved_recv[q]

    for copy in [*sum(x_copies, []), lift, panel_copy, *y_copies, *home_copies]:
        copy.wait_send()


def deliver_kernel(factor_ref, home_ref, factor_out, home_out, done):
    copies = [
        pltpu.make_async_copy(factor_ref, factor_out, done.at[0]),
        pltpu.make_async_copy(home_ref, home_out, done.at[1]),
    ]
    for copy in copies:
        copy.start()
    for copy in copies:
        copy.wait()


def body(diag_rows, next_rows, routes, diag_blocks, panel_blocks):
    x, y, diag, panel = diag_rows[0], next_rows[0], diag_blocks[0, 0], panel_blocks[0, 0]
    sources, width, depth = x.shape
    height = y.shape[1]
    columns = lax.axis_size("col")
    tiles = width // TILE
    kind = x.dtype
    vmem = pl.BlockSpec(memory_space=pltpu.VMEM)
    dma = pltpu.SemaphoreType.DMA
    factor, home = pl.pallas_call(
        level_kernel,
        out_shape=(
            jax.ShapeDtypeStruct((width, width), kind),
            jax.ShapeDtypeStruct((height, width), kind),
        ),
        in_specs=[vmem, vmem, pl.BlockSpec(memory_space=pltpu.SMEM), vmem, vmem],
        out_specs=(vmem, vmem),
        scratch_shapes=[
            pltpu.VMEM((columns - 1, width, depth), kind),
            pltpu.VMEM((columns, width, depth), kind),
            pltpu.VMEM((sources, height, depth), kind),
            pltpu.VMEM((columns - 1, height, depth), kind),
            pltpu.VMEM((columns, height, depth), kind),
            pltpu.VMEM((height, width), kind),
            pltpu.VMEM((tiles, height, TILE), kind),
            pltpu.VMEM((tiles, height, TILE), kind),
            pltpu.VMEM((width, width), jnp.float32),
            pltpu.VMEM((tiles, TILE, TILE), jnp.float32),
            pltpu.VMEM((TILE, 2 * TILE), jnp.float32),
            pltpu.VMEM((SMALL * SMALL, TILE), jnp.float32),
            dma((tiles, columns - 1)),
            dma((tiles, columns - 1)),
            dma((columns - 1,)),
            dma((columns - 1,)),
            dma((2,)),
            dma((2,)),
            dma((tiles,)),
            dma((tiles,)),
        ],
        compiler_params=pltpu.CompilerParams(
            collective_id=0, has_side_effects=True, vmem_limit_bytes=56 * 1024 * 1024
        ),
    )(x, y, routes[0, 0], diag, panel)
    anywhere = pl.BlockSpec(memory_space=pltpu.HBM)
    factor, home = pl.pallas_call(
        deliver_kernel,
        out_shape=(
            jax.ShapeDtypeStruct(factor.shape, kind),
            jax.ShapeDtypeStruct(home.shape, kind),
        ),
        in_specs=[anywhere, anywhere],
        out_specs=(anywhere, anywhere),
        scratch_shapes=[dma((2,))],
    )(factor, home)
    return (factor[None, None], home[None, None])


def solution(mesh):
    placed = (
        P("row", "col", None, None),
        P("row", "col", None, None),
        P("row", "col", None),
        P("row", "col", None, None),
        P("row", "col", None, None),
    )
    return jax.shard_map(
        body,
        mesh=mesh,
        in_specs=placed,
        out_specs=(P("row", "col", None, None), P("row", "col", None, None)),
        check_vma=False,
    )
```

```python
import jax
import jax.numpy as jnp
from jax import lax
from jax.experimental import pallas as pl
from jax.experimental.pallas import tpu as pltpu
from jax.sharding import PartitionSpec as P

TILE = 128
SMALL = 16
HALF = SMALL // 2
MESH = pl.DeviceIdType.MESH
NT = (((1,), (1,)), ((), ()))
TN = (((0,), (0,)), ((), ()))


def split(value):
    high = value.astype(jnp.bfloat16)
    low = (value - high.astype(jnp.float32)).astype(jnp.bfloat16)
    return high, low


def dot(left, right, dims):
    return lax.dot_general(left, right, dims, preferred_element_type=jnp.float32)


def product(left, right, axis, dims):
    left_high, left_low = split(left)
    right_high, right_low = split(right)
    return dot(
        jnp.concatenate([left_high, left_high, left_low], axis=axis),
        jnp.concatenate([right_high, right_low, right_high], axis=axis),
        dims,
    )


def eliminate(work, spread):
    full = (HALF, 2 * TILE)
    lane = lax.broadcasted_iota(jnp.int32, (SMALL, TILE), 1)

    def step(block, carry):
        start = pl.multiple_of(block * SMALL, SMALL)
        own = work.at[pl.ds(start, SMALL), :]
        pivots = pltpu.roll(own[:, :TILE], lax.rem(TILE - start, TILE), 1)
        tail = {}
        lower = {}
        for m in range(SMALL):
            wide = jnp.broadcast_to(pivots[:, m : m + 1], (SMALL, TILE))
            if m < HALF:
                spread[m * SMALL : m * SMALL + HALF, :] = wide[:HALF]
                lower[m] = wide[HALF:]
            else:
                tail[m] = wide[HALF:]
        rows = [jnp.broadcast_to(own[i : i + 1, :], full) for i in range(SMALL)]

        def single(m, i):
            at = m * SMALL + i
            return jnp.broadcast_to(spread[at : at + 1, :], (HALF, TILE))

        def twice(part):
            return jnp.concatenate([part, part], axis=1)

        for base in (0, HALF):
            inside = range(base, base + HALF)
            value = {(i, m): single(m, i) for m in inside for i in range(m, base + HALF)}
            for m in inside:
                scale = lax.rsqrt(value[m, m])
                column = {i: value[i, m] * scale for i in range(m + 1, base + HALF)}
                for k in column:
                    for i in range(k, base + HALF):
                        value[i, k] = value[i, k] - column[i] * column[k]
                rows[m] = rows[m] * twice(scale)
                own[m : m + 1, :] = rows[m][0:1, :]
                for k in column:
                    rows[k] = rows[k] - twice(column[k]) * rows[m]
                if base == 0:
                    lower[m] = lower[m] * scale
                    spread[m * SMALL + HALF : (m + 1) * SMALL, :] = lower[m]
                    for k in column:
                        lower[k] = lower[k] - column[k] * lower[m]
            if base == 0:
                for k in range(HALF, SMALL):
                    for m in range(HALF):
                        across = single(m, k)
                        tail[k] = tail[k] - across * lower[m]
                        rows[k] = rows[k] - twice(across) * rows[m]
                    spread[k * SMALL + HALF : (k + 1) * SMALL, :] = tail[k]
        solved = own[...]
        high, low = split(solved)
        left_high, left_low = split(jnp.where(lane >= start + SMALL, solved[:, :TILE], 0.0))
        update = dot(
            jnp.concatenate([left_high, left_high, left_low], axis=0),
            jnp.concatenate([high, low, high], axis=0),
            TN,
        )
        work[...] = work[...] - update
        return carry

    lax.fori_loop(0, TILE // SMALL, step, 0)


def level_kernel(
    x_ref, y_ref, routes_ref, diag_ref, panel_ref, factor_ref, home_ref,
    x_send, x_recv, y_lift, y_send, y_recv, panel_recv, solved_send, solved_recv,
    total, inverse, work, spread,
    x_out, x_in, y_out, y_in, row_out, row_in, home_out, home_in,
):
    sources, width, depth = x_ref.shape
    tiles = width // TILE
    columns, rows = lax.axis_size("col"), lax.axis_size("row")
    my_column, my_row = lax.axis_index("col"), lax.axis_index("row")
    ahead, behind = lax.rem(my_row + 1, rows), lax.rem(my_row + rows - 1, rows)
    partner = [lax.rem(my_column + d, columns) for d in range(columns)]

    barrier = pltpu.get_barrier_semaphore()
    for d in range(1, columns):
        pl.semaphore_signal(barrier, inc=1, device_id={"col": partner[d]}, device_id_type=MESH)
    for other in (ahead, behind):
        pl.semaphore_signal(barrier, inc=1, device_id={"row": other}, device_id_type=MESH)

    slot = []
    for d in range(columns):
        found = jnp.int32(0)
        for s in range(sources):
            found = jnp.where(routes_ref[s] == partner[d], jnp.int32(s), found)
        slot.append(found)

    def chunk(q):
        return slice(q * TILE, (q + 1) * TILE)

    def stage(q):
        for d in range(1, columns):
            x_send[d - 1, chunk(q), :] = x_ref[slot[d], chunk(q), :]
        x_recv[0, chunk(q), :] = x_ref[slot[0], chunk(q), :]

    def remote(source, target, out, into, device):
        return pltpu.make_async_remote_copy(
            src_ref=source, dst_ref=target, send_sem=out, recv_sem=into,
            device_id=device, device_id_type=MESH,
        )

    x_copies = [
        [
            remote(
                x_send.at[d - 1, chunk(q), :], x_recv.at[d, chunk(q), :],
                x_out.at[q, d - 1], x_in.at[q, d - 1], {"col": partner[d]},
            )
            for d in range(1, columns)
        ]
        for q in range(tiles)
    ]
    lift = remote(y_ref, y_lift, row_out.at[0], row_in.at[0], {"row": behind})
    panel_copy = remote(panel_ref, panel_recv, row_out.at[1], row_in.at[1], {"row": behind})
    y_copies = [
        remote(y_send.at[d - 1], y_recv.at[d], y_out.at[d - 1], y_in.at[d - 1], {"col": partner[d]})
        for d in range(1, columns)
    ]
    home_copies = [
        remote(
            solved_send.at[q], solved_recv.at[q], home_out.at[q], home_in.at[q], {"row": ahead}
        )
        for q in range(tiles)
    ]

    stage(0)
    pl.semaphore_wait(barrier, columns + 1)
    for copy in x_copies[0]:
        copy.start()
    lift.start()
    panel_copy.start()
    for q in range(1, tiles):
        stage(q)
        for copy in x_copies[q]:
            copy.start()

    row = lax.broadcasted_iota(jnp.int32, (TILE, TILE), 0)
    lane = lax.broadcasted_iota(jnp.int32, (TILE, TILE), 1)
    for q in range(tiles):
        low, high = q * TILE, (q + 1) * TILE
        for copy in x_copies[q]:
            copy.wait_recv()
        gram = diag_ref[low:high, :high].astype(jnp.float32)
        for s in range(columns):
            gram = gram + dot(x_recv[s, low:high, :], x_recv[s, :high, :], NT)
        total[low:high, :high] = gram
        for p in range(q):
            left = product(total[low:high, chunk(p)], inverse[p], 1, NT)
            total[low:high, chunk(p)] = left
            factor_ref[low:high, chunk(p)] = left.astype(jnp.bfloat16)
            total[low:high, (p + 1) * TILE : high] = total[
                low:high, (p + 1) * TILE : high
            ] - product(left, total[(p + 1) * TILE : high, chunk(p)], 1, NT)
        work[:, :TILE] = total[low:high, low:high]
        work[:, TILE:] = (row == lane).astype(jnp.float32)
        eliminate(work, spread)
        upper = jnp.where(row <= lane, work[:, :TILE], 0.0)
        factor_ref[low:high, low:high] = upper.T.astype(jnp.bfloat16)
        if q + 1 < tiles:
            factor_ref[low:high, high:] = jnp.zeros((TILE, width - high), jnp.bfloat16)
        inverse[q] = work[:, TILE:]
        if q == 0:
            lift.wait_recv()
            for d in range(1, columns):
                y_send[d - 1] = y_lift[slot[d]]
                y_copies[d - 1].start()
            y_recv[0] = y_lift[slot[0]]

    panel_copy.wait_recv()
    for copy in y_copies:
        copy.wait_recv()
    cross = panel_recv[...].astype(jnp.float32)
    for s in range(columns):
        cross = cross + dot(y_recv[s], x_recv[s], NT)
    for q in range(tiles):
        solved = product(cross[:, :TILE], inverse[q], 1, NT)
        solved_send[q] = solved.astype(jnp.bfloat16)
        home_copies[q].start()
        if q + 1 < tiles:
            cross = cross[:, TILE:] - product(solved, total[(q + 1) * TILE :, chunk(q)], 1, NT)
    for q in range(tiles):
        home_copies[q].wait_recv()
        home_ref[:, chunk(q)] = solved_recv[q]

    for copy in [*sum(x_copies, []), lift, panel_copy, *y_copies, *home_copies]:
        copy.wait_send()


def deliver_kernel(factor_ref, home_ref, factor_out, home_out, done):
    copies = [
        pltpu.make_async_copy(factor_ref, factor_out, done.at[0]),
        pltpu.make_async_copy(home_ref, home_out, done.at[1]),
    ]
    for copy in copies:
        copy.start()
    for copy in copies:
        copy.wait()


def body(diag_rows, next_rows, routes, diag_blocks, panel_blocks):
    x, y, diag, panel = diag_rows[0], next_rows[0], diag_blocks[0, 0], panel_blocks[0, 0]
    sources, width, depth = x.shape
    height = y.shape[1]
    columns = lax.axis_size("col")
    tiles = width // TILE
    kind = x.dtype
    vmem = pl.BlockSpec(memory_space=pltpu.VMEM)
    dma = pltpu.SemaphoreType.DMA
    factor, home = pl.pallas_call(
        level_kernel,
        out_shape=(
            jax.ShapeDtypeStruct((width, width), kind),
            jax.ShapeDtypeStruct((height, width), kind),
        ),
        in_specs=[vmem, vmem, pl.BlockSpec(memory_space=pltpu.SMEM), vmem, vmem],
        out_specs=(vmem, vmem),
        scratch_shapes=[
            pltpu.VMEM((columns - 1, width, depth), kind),
            pltpu.VMEM((columns, width, depth), kind),
            pltpu.VMEM((sources, height, depth), kind),
            pltpu.VMEM((columns - 1, height, depth), kind),
            pltpu.VMEM((columns, height, depth), kind),
            pltpu.VMEM((height, width), kind),
            pltpu.VMEM((tiles, height, TILE), kind),
            pltpu.VMEM((tiles, height, TILE), kind),
            pltpu.VMEM((width, width), jnp.float32),
            pltpu.VMEM((tiles, TILE, TILE), jnp.float32),
            pltpu.VMEM((TILE, 2 * TILE), jnp.float32),
            pltpu.VMEM((SMALL * SMALL, TILE), jnp.float32),
            dma((tiles, columns - 1)),
            dma((tiles, columns - 1)),
            dma((columns - 1,)),
            dma((columns - 1,)),
            dma((2,)),
            dma((2,)),
            dma((tiles,)),
            dma((tiles,)),
        ],
        compiler_params=pltpu.CompilerParams(
            collective_id=0, has_side_effects=True, vmem_limit_bytes=56 * 1024 * 1024
        ),
    )(x, y, routes[0, 0], diag, panel)
    anywhere = pl.BlockSpec(memory_space=pltpu.HBM)
    factor, home = pl.pallas_call(
        deliver_kernel,
        out_shape=(
            jax.ShapeDtypeStruct(factor.shape, kind),
            jax.ShapeDtypeStruct(home.shape, kind),
        ),
        in_specs=[vmem, vmem],
        out_specs=(anywhere, anywhere),
        scratch_shapes=[dma((2,))],
    )(factor, home)
    return (factor[None, None], home[None, None])


def solution(mesh):
    placed = (
        P("row", "col", None, None),
        P("row", "col", None, None),
        P("row", "col", None),
        P("row", "col", None, None),
        P("row", "col", None, None),
    )
    return jax.shard_map(
        body,
        mesh=mesh,
        in_specs=placed,
        out_specs=(P("row", "col", None, None), P("row", "col", None, None)),
        check_vma=False,
    )
```
